128 devices in a mesh: dp: 8 (over z, core), ctx: 16 (over y, x).
Axes of the slice: x: 4, y: 4, z: 4, core: 2. Of those that a mesh axis runs over, the one named last changes fastest.
Arguments:
- tokens: bfloat16 [8, 2048, 2240], P('dp', 'ctx'), may hold values from -6 to 6
- queries: bfloat16 [8, 2048, 2240], P('dp', 'ctx'), may hold values from -6 to 6
- cotangent: bfloat16 [8, 2048, 2240], P('dp', 'ctx'), may hold values from -6 to 6
- key_weight: bfloat16 [2240, 2240], P('ctx'), may hold values from -0.125 to 0.125
- value_weight: bfloat16 [2240, 2240], P('ctx'), may hold values from -0.125 to 0.125
- clip_len: int32 [8], P('dp'), may hold values from 512 to 2048, as said below
Outputs:
- grad_queries: bfloat16 [8, 2048, 2240], P('dp', 'ctx')
- grad_key_weight: float32 [2240, 2240], P('ctx')
The draws below stay inside these ranges and needn't reach their ends.
Inputs may be any that keep to these rules, and one draw needn't show every extreme that they name: `clip_len`: some clip has exactly 2048 live tokens.
All inputs are finite; a program needn't handle non-finite values.
Results may differ from the reference program's by a relative error of at most 0.02.
Values may be sent and summed in bfloat16 or wider, within the bound.
No kernel may reach another device: no remote copies, remote signals or barrier semaphores. Data moves between devices by JAX's collectives and lax.ppermute only.
A program may use at most 128 MiB of HBM per device.

```python
import jax
import jax.numpy as jnp
from jax import lax

HEADS = 20
HEAD_DIM = 112
D = 2240
TOKENS = 2048
CLIPS = 8


def draw_clip_len(key, part):
    first, second = jax.random.split(jax.random.fold_in(key, 7))
    lengths = jax.random.randint(first, (CLIPS,), TOKENS // 4, TOKENS + 1, dtype=jnp.int32)
    chosen = jax.random.randint(second, (), 0, CLIPS, dtype=jnp.int32)
    return jnp.where(jnp.arange(CLIPS, dtype=jnp.int32) == chosen, TOKENS, lengths).astype(jnp.int32)


def level_of(rng, shape, pieces, low, high):
    factor_of = 1.0
    for axis_at, parts in pieces:
        steps = jax.random.uniform(jax.random.fold_in(jax.random.fold_in(rng, 6), axis_at), (parts,), jnp.float32, low / len(pieces), high / len(pieces))
        factor_of = factor_of * jnp.repeat(jnp.exp(steps), shape[axis_at] // parts).reshape((-1,) + (1,) * (len(shape) - 1 - axis_at))
    return factor_of


def noise(own_key, shape, scale, most, cuts=(), kind=jnp.bfloat16):
    level = level_of(own_key, shape, cuts, -0.22, 0.18) if cuts else 1.0
    drawn = jax.random.normal(own_key, shape, jnp.float32) * scale * level
    return jnp.minimum(jnp.maximum(drawn, -most), most).astype(kind)


def setup_inputs(seed: int = 0) -> dict:
    key_list = jax.random.split(jax.random.key(seed), 7)
    return {
        "tokens": noise(key_list[0], (CLIPS, TOKENS, D), 1.0, 6.0, ((0, 8), (1, 16))),
        "queries": noise(key_list[1], (CLIPS, TOKENS, D), 1.0, 6.0, ((0, 8), (1, 16))),
        "cotangent": noise(key_list[2], (CLIPS, TOKENS, D), 1.0, 6.0, ((0, 8), (1, 16))),
        "key_weight": noise(key_list[3], (D, D), D ** -0.5, 0.125, ((0, 16),)),
        "value_weight": noise(key_list[4], (D, D), D ** -0.5, 0.125, ((0, 16),)),
        "clip_len": draw_clip_len(jax.random.fold_in(key_list[6], 71), 0),
    }


def one_clip(tokens, queries, cotangent, key_weight, value_weight, length):
    keys = jax.nn.relu(jnp.dot(tokens, key_weight, preferred_element_type=jnp.float32)).astype(jnp.bfloat16)
    values = jnp.dot(tokens, value_weight, preferred_element_type=jnp.float32).astype(jnp.bfloat16)
    live = (jnp.arange(TOKENS, dtype=jnp.int32) < length).astype(jnp.float32)[:, None, None]
    kf = keys.astype(jnp.float32).reshape(TOKENS, HEADS, HEAD_DIM)
    vf = values.astype(jnp.float32).reshape(TOKENS, HEADS, HEAD_DIM)
    summary = jnp.einsum("the,thf->hef", kf * live, vf)
    normer = jnp.sum(kf * live, axis=0)
    phi = jax.nn.relu(queries.astype(jnp.float32)).reshape(TOKENS, HEADS, HEAD_DIM)
    numer = jnp.einsum("the,hef->thf", phi, summary)
    denom = jnp.einsum("the,he->th", phi, normer) + length.astype(jnp.float32)
    back = cotangent.astype(jnp.float32).reshape(TOKENS, HEADS, HEAD_DIM) * live
    dnum = back / denom[:, :, None]
    dden = -jnp.sum(back * numer, axis=-1) / (denom * denom)
    dphi = jnp.einsum("thf,hef->the", dnum, summary) + dden[:, :, None] * normer[None]
    grad_q = (dphi * (phi > 0)).reshape(TOKENS, D).astype(jnp.bfloat16)
    dsummary = jnp.einsum("the,thf->hef", phi, dnum)
    dnormer = jnp.sum(phi * dden[:, :, None], axis=0)
    dkeys = (jnp.einsum("thf,hef->the", vf, dsummary) + dnormer[None]) * live * (kf > 0)
    dkeys = dkeys.reshape(TOKENS, D).astype(jnp.bfloat16)
    grad_w = lax.dot_general(tokens, dkeys, (((0,), (0,)), ((), ())), preferred_element_type=jnp.float32)
    return grad_q, grad_w


def reference(tokens, queries, cotangent, key_weight, value_weight, clip_len):
    grads = []
    total = jnp.zeros((D, D), jnp.float32)
    for clip in range(CLIPS):
        grad_q, grad_w = one_clip(tokens[clip], queries[clip], cotangent[clip], key_weight, value_weight, clip_len[clip])
        grads.append(grad_q)
        total = total + grad_w
    return jnp.stack(grads, axis=0), total
```

```python
import functools

import jax
import jax.numpy as jnp
from jax import lax
from jax.experimental import pallas as pl
from jax.experimental.pallas import tpu as pltpu
from jax.sharding import Mesh
from jax.sharding import PartitionSpec as P

HEADS = 20
HEAD_DIM = 112
D = 2240
NX = 4
NY = 4
NZ = 4
GH = HEADS // NX
GW = GH * HEAD_DIM
ROWS = 128
TOK = ROWS * NX
SH = D // 16
HALF = SH // 2
PAD = 72
SPLIT = 288
BF = jnp.bfloat16
F32 = jnp.float32
VMEM = pl.BlockSpec(memory_space=pltpu.VMEM)
SMEM = pl.BlockSpec(memory_space=pltpu.SMEM)
ANY = pl.BlockSpec(memory_space=pl.ANY)


def params():
    return pltpu.CompilerParams(vmem_limit_bytes=50 * 1024 * 1024)


def call(body, out_shape, in_specs, args, scratch=(), flops=0, nbytes=0, name=None):
    return pl.pallas_call(
        body,
        out_shape=out_shape,
        in_specs=in_specs,
        out_specs=jax.tree.map(lambda _: VMEM, out_shape),
        scratch_shapes=list(scratch),
        compiler_params=params(),
        cost_estimate=pl.CostEstimate(flops=flops, bytes_accessed=nbytes, transcendentals=0),
        name=name,
    )(*args)


def nt(a, b):
    return lax.dot_general(a, b, (((1,), (1,)), ((), ())), preferred_element_type=F32)


def tn(a, b):
    return lax.dot_general(a, b, (((0,), (0,)), ((), ())), preferred_element_type=F32)


def nn(a, b):
    return jnp.dot(a, b, preferred_element_type=F32)


def prep_weights(idx, wk, wv, out):
    for c, src in ((0, wk), (1, wv)):

        @pl.when(idx[1] == c)
        def _():
            for k in range(NX):
                out[k] = src[:, GW * k : GW * (k + 1)]


def prep_queries(idx, q, ct, *outs):
    for d in range(NX):
        for k in range(NX):

            @pl.when(lax.rem(idx[3] + d, NX) == k)
            def _():
                outs[d][0] = q[:, GW * k : GW * (k + 1)]
                outs[d][1] = ct[:, GW * k : GW * (k + 1)]


def live_mask(idx, width=TOK):
    pos = lax.broadcasted_iota(jnp.int32, (1, width), 1) + idx[2] * TOK
    return (pos < idx[4]).astype(F32)


def ones_row(v, row):
    pad = jnp.zeros((15, v.shape[1]), F32)
    return jnp.concatenate([v, row, pad], axis=0)


def project(idx, *refs):
    wblocks, tblocks = refs[:10], refs[10:15]
    kt, vt, summ, tfull, wbuf, sems = refs[15:]
    c, y, x = idx[1], idx[2], idx[3]
    copies = []

    def load(src, dst):
        cp = pltpu.make_async_copy(src, dst, sems.at[len(copies)])
        cp.start()
        copies.append(cp)

    def trow(off):
        return pl.ds(pl.multiple_of(lax.rem(x + off, NX) * ROWS, ROWS), ROWS)

    load(tblocks[0], tfull.at[trow(0)])
    load(tblocks[1], tfull.at[trow(3)])
    load(tblocks[2], tfull.at[trow(1)])
    base = pl.multiple_of(lax.rem(x + 2, NX) * ROWS, ROWS)
    load(tblocks[3], tfull.at[pl.ds(base, ROWS // 2)])
    load(tblocks[4], tfull.at[pl.ds(pl.multiple_of(base + ROWS // 2, ROWS // 2), ROWS // 2)])
    for g, blocks in ((c, wblocks[:5]), (1 - c, wblocks[5:])):
        dst = wbuf.at[g]

        def wrow(off, lo, size):
            start = lax.rem(y + off, NY) * GW + lo
            return pl.ds(pl.multiple_of(start, 16), size)

        load(blocks[0], dst.at[wrow(0, 0, GW)])
        load(blocks[1], dst.at[wrow(3, 0, GW)])
        load(blocks[2], dst.at[wrow(1, 0, GW)])
        load(blocks[3], dst.at[wrow(2, 0, SPLIT)])
        load(blocks[4], dst.at[wrow(2, SPLIT, GW - SPLIT)])
    for cp in copies:
        cp.wait()
    t = tfull[...]
    keys = jnp.maximum(nn(t, wbuf[0]), 0.0).T
    kt[...] = keys.astype(BF)
    vt[...] = nn(t, wbuf[1]).T.astype(BF)
    live = live_mask(idx)
    one = jnp.ones((1, TOK), F32)
    for h in range(GH):
        s = slice(HEAD_DIM * h, HEAD_DIM * (h + 1))
        kh = (kt[s].astype(F32) * live).astype(BF)
        vh = ones_row(vt[s].astype(F32), one).astype(BF)
        summ[s] = nt(kh, vh).astype(BF)


def query_side(idx, s0, s1, s2, s3, q0, q1, q2, q3, *refs):
    gq, dsum, qbuf, cbuf, gbuf, sems = refs[0:4], refs[4], refs[5], refs[6], refs[7], refs[8]
    x = idx[3]
    copies = []
    for d, src in enumerate((q0, q1, q2, q3)):
        rows = pl.ds(pl.multiple_of(lax.rem(x + d, NX) * ROWS, ROWS), ROWS)
        for k, dst in ((0, qbuf), (1, cbuf)):
            cp = pltpu.make_async_copy(src.at[k], dst.at[rows], sems.at[len(copies)])
            cp.start()
            copies.append(cp)
    summ = s0[...].astype(F32) + s1[...].astype(F32) + s2[...].astype(F32) + s3[...].astype(F32)
    live = live_mask(idx)
    length = idx[4].astype(F32)
    for cp in copies:
        cp.wait()
    qt = qbuf[...].astype(F32).T
    ct = cbuf[...].astype(F32).T
    grads = []
    for h in range(GH):
        s = slice(HEAD_DIM * h, HEAD_DIM * (h + 1))
        phi = jnp.maximum(qt[s], 0.0)
        phib = phi.astype(BF)
        back = ct[s] * live
        sh = summ[s].astype(BF)
        numer = tn(sh, phib)
        inv = 1.0 / (numer[HEAD_DIM : HEAD_DIM + 1] + length)
        dnum = back * inv
        dden = -jnp.sum(back * numer[:HEAD_DIM], axis=0, keepdims=True) * inv * inv
        ext = ones_row(dnum, dden).astype(BF)
        dphi = nn(sh, ext)
        grads.append(jnp.where(qt[s] > 0, dphi, 0.0))
        dsum[s] = nt(phib, ext).astype(BF)
    gbuf[...] = jnp.concatenate(grads, axis=0).T.astype(BF)
    for d in range(NX):
        rows = pl.ds(pl.multiple_of(lax.rem(x + d, NX) * ROWS, ROWS), ROWS)
        gq[d][...] = gbuf[rows]


def key_side(idx, s0, s1, s2, s3, kt, vt, dkt):
    summ = s0[...].astype(F32) + s1[...].astype(F32) + s2[...].astype(F32) + s3[...].astype(F32)
    summ = summ.astype(BF)
    live = live_mask(idx)
    one = jnp.ones((1, TOK), F32)
    for h in range(GH):
        s = slice(HEAD_DIM * h, HEAD_DIM * (h + 1))
        vh = ones_row(vt[s].astype(F32), one).astype(BF)
        dk = nn(summ[s], vh)
        keep = (kt[s].astype(F32) > 0) & (live > 0)
        dkt[s] = jnp.where(keep, dk, 0.0).astype(BF)


def transpose_tokens(idx, t, own, oth, buf):
    for k in range(0, D, 128):
        w = min(128, D - k)
        buf[k : k + w] = t[:, k : k + w].astype(F32).T
    zero = jnp.zeros((PAD - HALF, TOK), F32)
    for c in range(2):

        @pl.when(idx[1] == c)
        def _():
            for i in range(16):
                base = SH * ((i % 4) * 4 + i // 4)
                for half, dst in ((c, own), (1 - c, oth)):
                    lo = base + HALF * half
                    rows = jnp.concatenate([buf[lo : lo + HALF], zero], axis=0)
                    dst[PAD * i : PAD * (i + 1)] = rows.astype(BF)


def grad_weights(t_own, t_oth, d_own, d_oth, out):
    out[...] = (nt(t_own[...], d_own[...]) + nt(t_oth[...], d_oth[...])).astype(BF)


def sum_pieces(g, out):
    total = g[0].astype(F32)
    for i in range(1, 16):
        total = total + g[i].astype(F32)
    out[...] = total.astype(BF)


def place_rows(g, out):
    for z in range(NZ):
        for c in range(2):
            out[HALF * c : HALF * (c + 1), GW * z : GW * (z + 1)] = g[2 * z + c, :HALF].astype(F32)


def place_queries(idx, g0, g1, g2, g3, out):
    for d, src in enumerate((g0, g1, g2, g3)):
        for k in range(NX):

            @pl.when(lax.rem(idx[3] + d, NX) == k)
            def _():
                out[:, GW * k : GW * (k + 1)] = src[...]


def shift(v, axis, d, n=4):
    return lax.ppermute(v, axis, [(i, (i + d) % n) for i in range(n)])


def sds(shape, dtype=BF):
    return jax.ShapeDtypeStruct(shape, dtype)


def per_device(tokens, queries, cotangent, key_weight, value_weight, clip_len):
    z, c, y, x = (lax.axis_index(a) for a in ("z", "core", "y", "x"))
    idx = jnp.stack([z, c, y, x, clip_len[0]]).astype(jnp.int32)
    feats, quers, backs = tokens[0], queries[0], cotangent[0]

    def swap(v):
        return shift(v, "core", 1, 2)

    def sum_parts(s):
        return [s] + [shift(s, "y", d) for d in (1, 3, 2)]

    pieces = call(
        prep_weights, sds((NX, SH, GW)), [SMEM, VMEM, VMEM], (idx, key_weight, value_weight)
    )
    w_own = lax.all_to_all(pieces, "x", 0, 0, tiled=True).reshape(GW, GW)
    w_prev = shift(w_own, "y", 1)
    w_next = shift(w_own, "y", -1)
    t_prev = shift(feats, "x", 1)
    t_next = shift(feats, "x", -1)
    w_lo = shift(w_prev[:SPLIT], "y", 1)
    w_hi = shift(w_next[SPLIT:], "y", -1)
    t_lo = shift(t_prev[: ROWS // 2], "x", 1)
    t_hi = shift(t_next[ROWS // 2 :], "x", -1)
    blocks = [w_own, w_prev, w_next, w_lo, w_hi]
    blocks = blocks + [swap(b) for b in blocks]

    qc = call(
        prep_queries, [sds((2, ROWS, GW))] * NX, [SMEM, VMEM, VMEM], (idx, quers, backs)
    )
    q_in = [qc[0]]
    for d in (1, 2, 3):
        q_in.append(shift(qc[NX - d], "x", -d))

    kt, vt, summ, tfull = call(
        project,
        [sds((GW, TOK)), sds((GW, TOK)), sds((GW, 128)), sds((TOK, D))],
        [SMEM] + [ANY] * 15,
        (idx, *blocks, feats, t_prev, t_next, t_lo, t_hi),
        scratch=[pltpu.VMEM((2, D, GW), BF), pltpu.SemaphoreType.DMA((15,))],
        flops=4 * TOK * D * GW,
        nbytes=12_000_000,
    )
    t_own, t_oth = call(
        transpose_tokens,
        [sds((16 * PAD, TOK))] * 2,
        [SMEM, VMEM],
        (idx, tfull),
        scratch=[pltpu.VMEM((D, TOK), F32)],
        nbytes=10_000_000,
    )
    t_oth = swap(t_oth)

    outs = call(
        query_side,
        [sds((ROWS, GW))] * NX + [sds((GW, 128))],
        [SMEM] + [VMEM] * 4 + [ANY] * 4,
        (idx, *sum_parts(summ), *q_in),
        scratch=[pltpu.VMEM((TOK, GW), BF)] * 3 + [pltpu.SemaphoreType.DMA((8,))],
        flops=6 * TOK * GW * 128,
        nbytes=4_000_000,
    )
    gq, dsum = outs[:NX], outs[NX]
    g_in = [gq[0]]
    for d in (1, 2, 3):
        g_in.append(shift(gq[NX - d], "x", -d))
    dkt = call(
        key_side,
        sds((GW, TOK)),
        [SMEM] + [VMEM] * 6,
        (idx, *sum_parts(dsum), kt, vt),
        flops=2 * TOK * GW * 128,
        nbytes=2_000_000,
    )
    part = call(
        grad_weights,
        sds((16 * PAD, GW)),
        [VMEM] * 4,
        (t_own, t_oth, dkt, swap(dkt)),
        flops=4 * 16 * PAD * TOK * GW,
        nbytes=6_000_000,
    )
    part = lax.all_to_all(part.reshape(16, PAD, GW), ("z", "y"), 0, 0, tiled=True)
    rows = call(sum_pieces, sds((PAD, GW)), [VMEM], (part,))
    rows = lax.ppermute(rows, ("z", "x"), [(a * 4 + b, b * 4 + a) for a in range(4) for b in range(4)])
    rows = lax.all_gather(rows, ("z", "core"))
    grad_rows = call(place_rows, sds((SH, D), F32), [VMEM], (rows,))
    grad_q = call(place_queries, sds((ROWS, D)), [SMEM] + [VMEM] * 4, (idx, *g_in))
    return grad_q[None], grad_rows


def solution(mesh):
    grid = Mesh(mesh.devices.reshape(NZ, 2, NY, NX), ("z", "core", "y", "x"))
    dp, ctx = ("z", "core"), ("y", "x")
    in_specs = (
        P(dp, ctx, None),
        P(dp, ctx, None),
        P(dp, ctx, None),
        P(ctx, None),
        P(ctx, None),
        P(dp),
    )
    out_specs = (P(dp, ctx, None), P(ctx, None))
    return jax.shard_map(
        per_device, mesh=grid, in_specs=in_specs, out_specs=out_specs, check_vma=False
    )
```

```python
import jax
import jax.numpy as jnp
from jax import lax
from jax.experimental import pallas as pl
from jax.experimental.pallas import tpu as pltpu
from jax.sharding import Mesh
from jax.sharding import PartitionSpec as P

HEADS = 20
HEAD_DIM = 112
D = 2240
NX = 4
NY = 4
NZ = 4
GH = HEADS // NX
GW = GH * HEAD_DIM
ROWS = 128
TOK = ROWS * NX
SH = D // 16
HALF = SH // 2
PAD = 72
SPLIT = 288
BF = jnp.bfloat16
F32 = jnp.float32
VMEM = pl.BlockSpec(memory_space=pltpu.VMEM)
SMEM = pl.BlockSpec(memory_space=pltpu.SMEM)
ANY = pl.BlockSpec(memory_space=pl.ANY)
HBM = pl.BlockSpec(memory_space=pltpu.HBM)


def params(vmem):
    return pltpu.CompilerParams(vmem_limit_bytes=vmem * 1024 * 1024)


def call(body, out_shape, in_specs, args, scratch=(), flops=0, nbytes=0, name=None, vmem=6):
    return pl.pallas_call(
        body,
        out_shape=out_shape,
        in_specs=in_specs,
        out_specs=jax.tree.map(lambda _: VMEM, out_shape),
        scratch_shapes=list(scratch),
        compiler_params=params(vmem),
        cost_estimate=pl.CostEstimate(flops=flops, bytes_accessed=nbytes, transcendentals=0),
        name=name,
    )(*args)


def nt(a, b):
    return lax.dot_general(a, b, (((1,), (1,)), ((), ())), preferred_element_type=F32)


def tn(a, b):
    return lax.dot_general(a, b, (((0,), (0,)), ((), ())), preferred_element_type=F32)


def nn(a, b):
    return jnp.dot(a, b, preferred_element_type=F32)


def prep_weights(idx, wk, wv, out, buf, sem):
    for c, src in ((0, wk), (1, wv)):

        @pl.when(idx[1] == c)
        def _():
            cp = pltpu.make_async_copy(src, buf, sem)
            cp.start()
            cp.wait()

    for k in range(NX):
        out[k] = buf[:, GW * k : GW * (k + 1)]


def merge_weights(g, full):
    full[...] = jnp.concatenate([g[k].astype(F32) for k in range(NX)], axis=0).T.astype(BF)


def run_copies(pairs, sems):
    copies = [pltpu.make_async_copy(a, b, sems.at[i]) for i, (a, b) in enumerate(pairs)]
    for cp in copies:
        cp.start()
    return copies


def wait_all(copies):
    for cp in copies:
        cp.wait()


def prep_queries(idx, q, ct, o0, o1, o2, o3, sems):
    pairs = []
    for d, out in enumerate((o0, o1, o2, o3)):
        rows = pl.ds(pl.multiple_of(lax.rem(idx[3] + d, NX) * GW, 16), GW)
        pairs += [(q.at[rows], out.at[0]), (ct.at[rows], out.at[1])]
    wait_all(run_copies(pairs, sems))


def live_mask(idx, shift):
    lane = lax.broadcasted_iota(jnp.int32, (1, TOK), 1)
    block = lax.rem(shift + lane // ROWS, NX)
    pos = idx[2] * TOK + block * ROWS + lane % ROWS
    return (pos < idx[4]).astype(F32)


def ones_row(v, row):
    pad = jnp.zeros((15, v.shape[1]), F32)
    return jnp.concatenate([v, row, pad], axis=0)


def project(
    idx, w0, w_prev, w_next, w_lo, w_hi, v0, v_prev, v_next, v_lo, v_hi,
    t0, t1, t3, t2_lo, t2_hi, kt, vt, summ, tbuf, acc,
):
    for i, off in enumerate((0, 3, 1, 2)):
        block = lax.rem(idx[2] + off, NY)
        start = pl.multiple_of(block * GW, 16)
        for d, t in ((0, t0), (1, t1), (3, t3)):
            tbuf[i, :, ROWS * d : ROWS * (d + 1)] = t[pl.ds(start, GW)]
        near = pl.multiple_of(lax.rem(block, 2) * GW, 16)
        for lo, t in ((True, t2_lo), (False, t2_hi)):

            @pl.when((block < 2) == lo)
            def _():
                tbuf[i, :, 2 * ROWS : 3 * ROWS] = t[pl.ds(near, GW)]

    c = idx[1]
    for g, ws in ((c, (w0, w_prev, w_next)), (1 - c, (v0, v_prev, v_next))):
        lo, hi = (w_lo, w_hi) if ws[0] is w0 else (v_lo, v_hi)
        far = jnp.concatenate([lo[...], hi[...]], axis=0)
        total = nn(far, tbuf[3])
        for i, w in enumerate(ws):
            total = total + nn(w[...], tbuf[i])
        acc[g] = total.astype(BF)
    live = live_mask(idx, idx[3])
    one = jnp.ones((1, TOK), F32)
    for h in range(GH):
        s = slice(HEAD_DIM * h, HEAD_DIM * (h + 1))
        keys = jnp.maximum(acc[0, s].astype(F32), 0.0)
        values = acc[1, s]
        kt[s] = keys.astype(BF)
        vt[s] = values
        vh = ones_row(values.astype(F32), one).astype(BF)
        summ[s] = nt((keys * live).astype(BF), vh).astype(BF)


def total_of(parts):
    total = parts[0][...].astype(F32)
    for p in parts[1:]:
        total = total + p[...].astype(F32)
    return total.astype(BF)


def query_side(idx, s0, s1, s2, s3, q0, q1, q2, q3, g0, g1, g2, g3, dsum):
    summ = total_of((s0, s1, s2, s3))
    live = live_mask(idx, idx[3])
    qc = (q0, q1, q2, q3)
    length = idx[4].astype(F32)
    for h in range(GH):
        s = slice(HEAD_DIM * h, HEAD_DIM * (h + 1))
        q = jnp.concatenate([r[0, s].astype(F32) for r in qc], axis=1)
        back = jnp.concatenate([r[1, s].astype(F32) for r in qc], axis=1) * live
        phi = jnp.maximum(q, 0.0)
        phib = phi.astype(BF)
        sh = summ[s]
        numer = tn(sh, phib)
        inv = 1.0 / (numer[HEAD_DIM : HEAD_DIM + 1] + length)
        dnum = back * inv
        dden = -jnp.sum(back * numer[:HEAD_DIM], axis=0, keepdims=True) * inv * inv
        ext = ones_row(dnum, dden).astype(BF)
        grad = jnp.where(q > 0, nn(sh, ext), 0.0).astype(BF)
        for d, g in enumerate((g0, g1, g2, g3)):
            g[s] = grad[:, ROWS * d : ROWS * (d + 1)]
        dsum[s] = nt(phib, ext).astype(BF)


def key_side(idx, s0, s1, s2, s3, kt, vt, dkt):
    summ = total_of((s0, s1, s2, s3))
    live = live_mask(idx, idx[3])
    one = jnp.ones((1, TOK), F32)
    for h in range(GH):
        s = slice(HEAD_DIM * h, HEAD_DIM * (h + 1))
        vh = ones_row(vt[s].astype(F32), one).astype(BF)
        dk = nn(summ[s], vh)
        keep = (kt[s].astype(F32) > 0) & (live > 0)
        dkt[s] = jnp.where(keep, dk, 0.0).astype(BF)


def group_tokens(idx, t0, t1, t3, t2_lo, t2_hi, own, oth, buf):
    for d, t in ((0, t0), (1, t1), (3, t3)):
        buf[:, ROWS * d : ROWS * (d + 1)] = t[...].astype(F32)
    buf[: D // 2, 2 * ROWS : 3 * ROWS] = t2_lo[...].astype(F32)
    buf[D // 2 :, 2 * ROWS : 3 * ROWS] = t2_hi[...].astype(F32)
    zero = jnp.zeros((PAD - HALF, TOK), F32)
    for c in range(2):

        @pl.when(idx[1] == c)
        def _():
            for i in range(16):
                base = SH * i
                for half, dst in ((c, own), (1 - c, oth)):
                    lo = base + HALF * half
                    rows = jnp.concatenate([buf[lo : lo + HALF], zero], axis=0)
                    dst[PAD * i : PAD * (i + 1)] = rows.astype(BF)


def grad_weights(idx, t_own, t_oth, d_own, d_oth, out):
    part = (nt(t_own[...], d_own[...]) + nt(t_oth[...], d_oth[...])).astype(BF)
    for y in range(NY):
        for x in range(NX):
            i = NX * y + x
            z = lax.rem(x - idx[3] + NX, NX)
            out[z * NY + y] = part[PAD * i : PAD * (i + 1)]


def sum_pieces(g, out):
    total = g[0].astype(F32)
    for i in range(1, 16):
        total = total + g[i].astype(F32)
    out[...] = total.astype(BF)


def place_rows(idx, r0, r1, r2, r3, o0, o1, o2, o3, out):
    for c in range(2):
        for k in range(NX):
            for step, (r, o) in enumerate(((r0, o0), (r1, o1), (r2, o2), (r3, o3))):

                @pl.when((idx[1] == c) & (lax.rem(idx[3] - idx[0] + step + NX, NX) == k))
                def _():
                    cols = slice(GW * k, GW * (k + 1))
                    out[HALF * c : HALF * (c + 1), cols] = r[:HALF].astype(F32)
                    out[HALF * (1 - c) : HALF * (2 - c), cols] = o[:HALF].astype(F32)


def place_queries(idx, g0, g1, g2, g3, out):
    for d, src in enumerate((g0, g1, g2, g3)):
        out[pl.ds(pl.multiple_of(lax.rem(idx[3] + d, NX) * GW, 16), GW)] = src[...]


def shift(v, axis, d, n=4):
    return lax.ppermute(v, axis, [(i, (i + d) % n) for i in range(n)])


def sds(shape, dtype=BF):
    return jax.ShapeDtypeStruct(shape, dtype)


def per_device(tokens, queries, cotangent, key_weight, value_weight, clip_len):
    z, c, y, x = (lax.axis_index(a) for a in ("z", "core", "y", "x"))
    idx = jnp.stack([z, c, y, x, clip_len[0]]).astype(jnp.int32)
    t_own, quers, backs = tokens[0].T, queries[0].T, cotangent[0].T

    def swap(v):
        return shift(v, "core", 1, 2)

    def sum_parts(s):
        return [s] + [shift(s, "y", d) for d in (1, 3, 2)]

    pieces = call(
        prep_weights,
        sds((NX, SH, GW)),
        [SMEM, HBM, HBM],
        (idx, key_weight, value_weight),
        scratch=[pltpu.VMEM((SH, D), BF), pltpu.SemaphoreType.DMA],
        vmem=60,
    )
    merged = lax.all_to_all(pieces, "x", 0, 0, tiled=True)
    t_own, _ = lax.optimization_barrier((t_own, pieces))
    qc = call(
        prep_queries,
        [sds((2, GW, ROWS))] * NX,
        [SMEM, ANY, ANY],
        (idx, quers, backs),
        scratch=[pltpu.SemaphoreType.DMA((8,))],
    )
    merged, *qc = lax.optimization_barrier((merged, *qc))
    w_own = call(merge_weights, sds((GW, GW)), [VMEM], (merged,))
    w_prev = shift(w_own, "y", 1)
    w_next = shift(w_own, "y", -1)
    t_prev = shift(t_own, "x", 1)
    t_next = shift(t_own, "x", -1)
    f_lo = shift(w_prev[:SPLIT], "y", 1)
    f_hi = shift(w_next[SPLIT:], "y", -1)
    t_lo = shift(t_prev[: D // 2], "x", 1)
    t_hi = shift(t_next[D // 2 :], "x", -1)
    ts = (t_own, t_next, t_prev, t_lo, t_hi)
    g_own, g_oth = call(
        group_tokens,
        [sds((16 * PAD, TOK))] * 2,
        [SMEM] + [VMEM] * 5,
        (idx, *ts),
        scratch=[pltpu.VMEM((D, TOK), F32)],
        vmem=10,
        nbytes=10_000_000,
    )
    f_lo, f_hi, g_own, g_oth = lax.optimization_barrier((f_lo, f_hi, g_own, g_oth))
    ws = (w_own, w_prev, w_next, f_lo, f_hi)
    kt, vt, summ = call(
        project,
        [sds((GW, TOK)), sds((GW, TOK)), sds((GW, 128))],
        [SMEM] + [VMEM] * 15,
        (idx, *ws, *[swap(w) for w in ws], *ts),
        scratch=[pltpu.VMEM((NY, GW, TOK), BF), pltpu.VMEM((2, GW, TOK), BF)],
        vmem=16,
        flops=4 * TOK * D * GW,
        nbytes=5_000_000,
    )
    summ, *qc = lax.optimization_barrier((summ, *qc))
    parts = sum_parts(summ)
    q_in = [qc[0]] + [shift(qc[NX - d], "x", -d) for d in (1, 2, 3)]
    g_oth = swap(g_oth)

    outs = call(
        query_side,
        [sds((GW, ROWS))] * NX + [sds((GW, 128))],
        [SMEM] + [VMEM] * 8,
        (idx, *parts, *q_in),
        flops=6 * TOK * GW * 128,
        nbytes=4_000_000,
    )
    gq, dsum = outs[:NX], outs[NX]
    parts = sum_parts(dsum)
    g_in = [gq[0]]
    for d in (1, 2, 3):
        g_in.append(shift(gq[NX - d], "x", -d))
    dkt = call(
        key_side,
        sds((GW, TOK)),
        [SMEM] + [VMEM] * 6,
        (idx, *parts, kt, vt),
        flops=2 * TOK * GW * 128,
        nbytes=2_000_000,
    )
    part = call(
        grad_weights,
        sds((16, PAD, GW)),
        [SMEM] + [VMEM] * 4,
        (idx, g_own, g_oth, dkt, swap(dkt)),
        flops=4 * 16 * PAD * TOK * GW,
        nbytes=6_000_000,
    )
    part = lax.all_to_all(part, ("z", "y"), 0, 0, tiled=True)
    grad_q = call(place_queries, sds((D, ROWS)), [SMEM] + [VMEM] * 4, (idx, *g_in))
    part, grad_q = lax.optimization_barrier((part, grad_q))
    rows = call(sum_pieces, sds((PAD, GW)), [VMEM], (part,))
    got = [
        lax.ppermute(
            rows,
            ("z", "x"),
            [
                (z_at * NX + x_at, (z_at + s) % NZ * NX + (x_at + z_at) % NX)
                for z_at in range(NZ)
                for x_at in range(NX)
            ],
        )
        for s in range(NZ)
    ]
    grad_rows = call(
        place_rows, sds((SH, D), F32), [SMEM] + [VMEM] * 8, (idx, *got, *[swap(g) for g in got])
    )
    return grad_q.T[None], grad_rows


def solution(mesh):
    grid = Mesh(mesh.devices.reshape(NZ, 2, NY, NX), ("z", "core", "y", "x"))
    dp, ctx = ("z", "core"), ("y", "x")
    in_specs = (
        P(dp, ctx, None),
        P(dp, ctx, None),
        P(dp, ctx, None),
        P(ctx, None),
        P(ctx, None),
        P(dp),
    )
    out_specs = (P(dp, ctx, None), P(ctx, None))
    return jax.shard_map(
        per_device, mesh=grid, in_specs=in_specs, out_specs=out_specs, check_vma=False
    )
```

```python
import jax
import jax.numpy as jnp
from jax import lax
from jax.experimental import pallas as pl
from jax.experimental.pallas import tpu as pltpu
from jax.sharding import Mesh
from jax.sharding import PartitionSpec as P

HEADS = 20
HEAD_DIM = 112
D = 2240
NX = 4
NY = 4
NZ = 4
GH = HEADS // NX
GW = GH * HEAD_DIM
ROWS = 128
TOK = ROWS * NX
SH = D // 16
HALF = SH // 2
PAD = 72
SPLIT = 288
BF = jnp.bfloat16
F32 = jnp.float32
VMEM = pl.BlockSpec(memory_space=pltpu.VMEM)
SMEM = pl.BlockSpec(memory_space=pltpu.SMEM)
ANY = pl.BlockSpec(memory_space=pl.ANY)
HBM = pl.BlockSpec(memory_space=pltpu.HBM)


def params(vmem):
    return pltpu.CompilerParams(vmem_limit_bytes=vmem * 1024 * 1024)


def call(body, out_shape, in_specs, args, scratch=(), flops=0, nbytes=0, name=None, vmem=6):
    return pl.pallas_call(
        body,
        out_shape=out_shape,
        in_specs=in_specs,
        out_specs=jax.tree.map(lambda _: VMEM, out_shape),
        scratch_shapes=list(scratch),
        compiler_params=params(vmem),
        cost_estimate=pl.CostEstimate(flops=flops, bytes_accessed=nbytes, transcendentals=0),
        name=name,
    )(*args)


def nt(a, b):
    return lax.dot_general(a, b, (((1,), (1,)), ((), ())), preferred_element_type=F32)


def tn(a, b):
    return lax.dot_general(a, b, (((0,), (0,)), ((), ())), preferred_element_type=F32)


def nn(a, b):
    return jnp.dot(a, b, preferred_element_type=F32)


def prep_weights(wk, wv, out, buf, sem):
    core = lax.axis_index("core")
    for c, src in ((0, wk), (1, wv)):

        @pl.when(core == c)
        def _():
            cp = pltpu.make_async_copy(src, buf, sem)
            cp.start()
            cp.wait()

    for k in range(NX):
        out[k] = buf[:, GW * k : GW * (k + 1)]


def merge_weights(g, full):
    full[...] = jnp.concatenate([g[k].astype(F32) for k in range(NX)], axis=0).T.astype(BF)


def run_copies(pairs, sems):
    copies = [pltpu.make_async_copy(a, b, sems.at[i]) for i, (a, b) in enumerate(pairs)]
    for cp in copies:
        cp.start()
    return copies


def wait_all(copies):
    for cp in copies:
        cp.wait()


def prep_queries(idx, q, ct, o0, o1, o2, o3, sems):
    pairs = []
    for d, out in enumerate((o0, o1, o2, o3)):
        rows = pl.ds(pl.multiple_of(lax.rem(idx[3] + d, NX) * GW, 16), GW)
        pairs += [(q.at[rows], out.at[0]), (ct.at[rows], out.at[1])]
    wait_all(run_copies(pairs, sems))


def live_mask(idx, shift):
    lane = lax.broadcasted_iota(jnp.int32, (1, TOK), 1)
    block = lax.rem(shift + lane // ROWS, NX)
    pos = idx[2] * TOK + block * ROWS + lane % ROWS
    return (pos < idx[4]).astype(F32)


def ones_row(v, row):
    pad = jnp.zeros((15, v.shape[1]), F32)
    return jnp.concatenate([v, row, pad], axis=0)


def project(
    idx, w0, w_prev, w_next, w_lo, w_hi, v0, v_prev, v_next, v_lo, v_hi,
    t0, t1, t3, t2_lo, t2_hi, kt, vt, summ, tbuf, acc,
):
    for i, off in enumerate((0, 3, 1, 2)):
        block = lax.rem(idx[2] + off, NY)
        start = pl.multiple_of(block * GW, 16)
        for d, t in ((0, t0), (1, t1), (3, t3)):
            tbuf[i, :, ROWS * d : ROWS * (d + 1)] = t[pl.ds(start, GW)]
        near = pl.multiple_of(lax.rem(block, 2) * GW, 16)
        for lo, t in ((True, t2_lo), (False, t2_hi)):

            @pl.when((block < 2) == lo)
            def _():
                tbuf[i, :, 2 * ROWS : 3 * ROWS] = t[pl.ds(near, GW)]

    c = idx[1]
    for g, ws in ((c, (w0, w_prev, w_next)), (1 - c, (v0, v_prev, v_next))):
        lo, hi = (w_lo, w_hi) if ws[0] is w0 else (v_lo, v_hi)
        far = jnp.concatenate([lo[...], hi[...]], axis=0)
        total = nn(far, tbuf[3])
        for i, w in enumerate(ws):
            total = total + nn(w[...], tbuf[i])
        acc[g] = total.astype(BF)
    live = live_mask(idx, idx[3])
    one = jnp.ones((1, TOK), F32)
    for h in range(GH):
        s = slice(HEAD_DIM * h, HEAD_DIM * (h + 1))
        keys = jnp.maximum(acc[0, s].astype(F32), 0.0)
        values = acc[1, s]
        kt[s] = keys.astype(BF)
        vt[s] = values
        vh = ones_row(values.astype(F32), one).astype(BF)
        summ[s] = nt((keys * live).astype(BF), vh).astype(BF)


def total_of(parts):
    total = parts[0][...].astype(F32)
    for p in parts[1:]:
        total = total + p[...].astype(F32)
    return total.astype(BF)


def query_side(idx, s0, s1, s2, s3, q0, q1, q2, q3, g0, g1, g2, g3, dsum):
    summ = total_of((s0, s1, s2, s3))
    live = live_mask(idx, idx[3])
    length = idx[4].astype(F32)
    for h in range(GH):
        s = slice(HEAD_DIM * h, HEAD_DIM * (h + 1))

        def pieces(k):
            at = slice(D // 2 + GW * k + s.start, D // 2 + GW * k + s.stop)
            parts = (q0[k, s], q1[at], q2[k, s], q3[at])
            return jnp.concatenate([p.astype(F32) for p in parts], axis=1)

        q = pieces(0)
        back = pieces(1) * live
        phi = jnp.maximum(q, 0.0)
        phib = phi.astype(BF)
        sh = summ[s]
        numer = tn(sh, phib)
        inv = 1.0 / (numer[HEAD_DIM : HEAD_DIM + 1] + length)
        dnum = back * inv
        dden = -jnp.sum(back * numer[:HEAD_DIM], axis=0, keepdims=True) * inv * inv
        ext = ones_row(dnum, dden).astype(BF)
        grad = jnp.where(q > 0, nn(sh, ext), 0.0).astype(BF)
        for d, g in enumerate((g0, g1, g2, g3)):
            g[s] = grad[:, ROWS * d : ROWS * (d + 1)]
        dsum[s] = nt(phib, ext).astype(BF)


def key_side(idx, s0, s1, s2, s3, kt, vt, dkt):
    summ = total_of((s0, s1, s2, s3))
    live = live_mask(idx, idx[3])
    one = jnp.ones((1, TOK), F32)
    for h in range(GH):
        s = slice(HEAD_DIM * h, HEAD_DIM * (h + 1))
        vh = ones_row(vt[s].astype(F32), one).astype(BF)
        dk = nn(summ[s], vh)
        keep = (kt[s].astype(F32) > 0) & (live > 0)
        dkt[s] = jnp.where(keep, dk, 0.0).astype(BF)


def group_tokens(idx, t0, t1, t3, t2_lo, t2_hi, own, oth, buf):
    for d, t in ((0, t0), (1, t1), (3, t3)):
        buf[:, ROWS * d : ROWS * (d + 1)] = t[...].astype(F32)
    buf[: D // 2, 2 * ROWS : 3 * ROWS] = t2_lo[: D // 2].astype(F32)
    buf[D // 2 :, 2 * ROWS : 3 * ROWS] = t2_hi[: D // 2].astype(F32)
    zero = jnp.zeros((PAD - HALF, TOK), F32)
    for c in range(2):

        @pl.when(idx[1] == c)
        def _():
            for i in range(16):
                base = SH * i
                for half, dst in ((c, own), (1 - c, oth)):
                    lo = base + HALF * half
                    rows = jnp.concatenate([buf[lo : lo + HALF], zero], axis=0)
                    dst[PAD * i : PAD * (i + 1)] = rows.astype(BF)


def grad_first(t, d, out):
    out[...] = nt(t[...], d[...])


def grad_second(idx, first, t, d, out):
    part = (first[...] + nt(t[...], d[...])).astype(BF)
    for y in range(NY):
        for x in range(NX):
            i = NX * y + x
            z = lax.rem(x - idx[3] + NX, NX)
            out[z * NY + y] = part[PAD * i : PAD * (i + 1)]


def sum_pieces(g, out):
    total = g[0].astype(F32)
    for i in range(1, 16):
        total = total + g[i].astype(F32)
    out[...] = total.astype(BF)


def place_rows(idx, r0, r1, r2, r3, o0, o1, o2, o3, out, buf):
    for step, (r, o) in enumerate(((r0, o0), (r1, o1), (r2, o2), (r3, o3))):
        k = lax.rem(idx[3] - idx[0] + step + NX, NX)
        buf[idx[1], k] = r[...].astype(F32)
        buf[1 - idx[1], k] = o[...].astype(F32)
    for c in range(2):
        for k in range(NX):
            out[HALF * c : HALF * (c + 1), GW * k : GW * (k + 1)] = buf[c, k, :HALF]


def place_queries(idx, g0, g1, g2, g3, out):
    for d, src in enumerate((g0, g1, g2, g3)):
        out[pl.ds(pl.multiple_of(lax.rem(idx[3] + d, NX) * GW, 16), GW)] = src[...]


def shift(v, axis, d, n=4):
    return lax.ppermute(v, axis, [(i, (i + d) % n) for i in range(n)])


def sds(shape, dtype=BF):
    return jax.ShapeDtypeStruct(shape, dtype)


def per_device(tokens, queries, cotangent, key_weight, value_weight, clip_len):
    z, c, y, x = (lax.axis_index(a) for a in ("z", "core", "y", "x"))
    idx = jnp.stack([z, c, y, x, clip_len[0]]).astype(jnp.int32)
    t_own, quers, backs = tokens[0].T, queries[0].T, cotangent[0].T

    def swap(v):
        return shift(v, "core", 1, 2)

    def sum_parts(s):
        return [s] + [shift(s, "y", d) for d in (1, 3, 2)]

    pieces = call(
        prep_weights,
        sds((NX, SH, GW)),
        [HBM, HBM],
        (key_weight, value_weight),
        scratch=[pltpu.VMEM((SH, D), BF), pltpu.SemaphoreType.DMA],
        vmem=60,
    )
    merged = lax.all_to_all(pieces, "x", 0, 0, tiled=True)
    t_own, _ = lax.optimization_barrier((t_own, pieces))
    qc = call(
        prep_queries,
        [sds((2, GW, ROWS))] * NX,
        [SMEM, ANY, ANY],
        (idx, quers, backs),
        scratch=[pltpu.SemaphoreType.DMA((8,))],
    )
    merged, *qc = lax.optimization_barrier((merged, *qc))
    t_late, _ = lax.optimization_barrier((t_own, merged))
    w_own = call(merge_weights, sds((GW, GW)), [VMEM], (merged,))
    w_prev = shift(w_own, "y", 1)
    w_next = shift(w_own, "y", -1)
    t_prev = shift(t_late, "x", 1)
    t_next = shift(t_own, "x", -1)
    f_lo = shift(w_prev[:SPLIT], "y", 1)
    f_hi = shift(w_next[SPLIT:], "y", -1)
    t_lo = shift(jnp.concatenate([t_prev[: D // 2], qc[1].reshape(2 * GW, ROWS)]), "x", 1)
    t_hi = shift(jnp.concatenate([t_next[D // 2 :], qc[3].reshape(2 * GW, ROWS)]), "x", -1)
    ts = (t_own, t_next, t_prev, t_lo, t_hi)
    g_own, g_oth = call(
        group_tokens,
        [sds((16 * PAD, TOK))] * 2,
        [SMEM] + [VMEM] * 5,
        (idx, *ts),
        scratch=[pltpu.VMEM((D, TOK), F32)],
        vmem=10,
        nbytes=10_000_000,
    )
    f_lo, f_hi, g_own, g_oth = lax.optimization_barrier((f_lo, f_hi, g_own, g_oth))
    ws = (w_own, w_prev, w_next, f_lo, f_hi)
    kt, vt, summ = call(
        project,
        [sds((GW, TOK)), sds((GW, TOK)), sds((GW, 128))],
        [SMEM] + [VMEM] * 15,
        (idx, *ws, *[swap(w) for w in ws], *ts),
        scratch=[pltpu.VMEM((NY, GW, TOK), BF), pltpu.VMEM((2, GW, TOK), BF)],
        vmem=16,
        flops=4 * TOK * D * GW,
        nbytes=5_000_000,
    )
    summ, far = lax.optimization_barrier((summ, qc[2]))
    parts = sum_parts(summ)
    q_in = (qc[0], t_hi, shift(far, "x", 2), t_lo)
    g_oth = swap(g_oth)

    outs = call(
        query_side,
        [sds((GW, ROWS))] * NX + [sds((GW, 128))],
        [SMEM] + [VMEM] * 8,
        (idx, *parts, *q_in),
        flops=6 * TOK * GW * 128,
        nbytes=4_000_000,
    )
    gq, dsum = outs[:NX], outs[NX]
    parts = sum_parts(dsum)
    g_in = [gq[0]]
    for d in (1, 2, 3):
        g_in.append(shift(gq[NX - d], "x", -d))
    dkt = call(
        key_side,
        sds((GW, TOK)),
        [SMEM] + [VMEM] * 6,
        (idx, *parts, kt, vt),
        flops=2 * TOK * GW * 128,
        nbytes=2_000_000,
    )
    first = call(
        grad_first,
        sds((16 * PAD, GW), F32),
        [VMEM] * 2,
        (g_own, dkt),
        flops=2 * 16 * PAD * TOK * GW,
        nbytes=5_000_000,
    )
    part = call(
        grad_second,
        sds((16, PAD, GW)),
        [SMEM] + [VMEM] * 3,
        (idx, first, g_oth, swap(dkt)),
        flops=2 * 16 * PAD * TOK * GW,
        nbytes=5_000_000,
    )
    part = lax.all_to_all(part, ("z", "y"), 0, 0, tiled=True)
    grad_q = call(place_queries, sds((D, ROWS)), [SMEM] + [VMEM] * 4, (idx, *g_in))
    part, grad_q = lax.optimization_barrier((part, grad_q))
    rows = call(sum_pieces, sds((PAD, GW)), [VMEM], (part,))
    got = [
        lax.ppermute(
            rows,
            ("z", "x"),
            [
                (z_at * NX + x_at, (z_at + s) % NZ * NX + (x_at + z_at) % NX)
                for z_at in range(NZ)
                for x_at in range(NX)
            ],
        )
        for s in range(NZ)
    ]
    grad_rows = call(
        place_rows,
        sds((SH, D), F32),
        [SMEM] + [VMEM] * 8,
        (idx, *got, *[swap(g) for g in got]),
        scratch=[pltpu.VMEM((2, NX, PAD, GW), F32)],
    )
    return grad_q.T[None], grad_rows


def solution(mesh):
    grid = Mesh(mesh.devices.reshape(NZ, 2, NY, NX), ("z", "core", "y", "x"))
    dp, ctx = ("z", "core"), ("y", "x")
    in_specs = (
        P(dp, ctx, None),
        P(dp, ctx, None),
        P(dp, ctx, None),
        P(ctx, None),
        P(ctx, None),
        P(dp),
    )
    out_specs = (P(dp, ctx, None), P(ctx, None))
    return jax.shard_map(
        per_device, mesh=grid, in_specs=in_specs, out_specs=out_specs, check_vma=False
    )
```

```python
import jax
import jax.numpy as jnp
from jax import lax
from jax.experimental import pallas as pl
from jax.experimental.pallas import tpu as pltpu
from jax.sharding import Mesh
from jax.sharding import PartitionSpec as P

HEADS = 20
HEAD_DIM = 112
D = 2240
NX = 4
NY = 4
NZ = 4
GH = HEADS // NX
GW = GH * HEAD_DIM
ROWS = 128
TOK = ROWS * NX
SH = D // 16
HALF = SH // 2
PAD = 72
PR, PL = 64, 640
EX = PL - GW
SPLIT = 288
BF = jnp.bfloat16
F32 = jnp.float32
VMEM = pl.BlockSpec(memory_space=pltpu.VMEM)
SMEM = pl.BlockSpec(memory_space=pltpu.SMEM)
ANY = pl.BlockSpec(memory_space=pl.ANY)
HBM = pl.BlockSpec(memory_space=pltpu.HBM)


def params(vmem):
    return pltpu.CompilerParams(vmem_limit_bytes=vmem * 1024 * 1024)


def call(body, out_shape, in_specs, args, scratch=(), flops=0, nbytes=0, name=None, vmem=6):
    return pl.pallas_call(
        body,
        out_shape=out_shape,
        in_specs=in_specs,
        out_specs=jax.tree.map(lambda _: VMEM, out_shape),
        scratch_shapes=list(scratch),
        compiler_params=params(vmem),
        cost_estimate=pl.CostEstimate(flops=flops, bytes_accessed=nbytes, transcendentals=0),
        name=name,
    )(*args)


def nt(a, b):
    return lax.dot_general(a, b, (((1,), (1,)), ((), ())), preferred_element_type=F32)


def tn(a, b):
    return lax.dot_general(a, b, (((0,), (0,)), ((), ())), preferred_element_type=F32)


def nn(a, b):
    return jnp.dot(a, b, preferred_element_type=F32)


def prep_weights(wk, wv, out, buf, sem):
    core = lax.axis_index("core")
    for c, src in ((0, wk), (1, wv)):

        @pl.when(core == c)
        def _():
            cp = pltpu.make_async_copy(src, buf, sem)
            cp.start()
            cp.wait()

    for k in range(NX):
        out[k] = buf[:, GW * k : GW * (k + 1)]


def merge_weights(g, full):
    full[...] = jnp.concatenate([g[k].astype(F32) for k in range(NX)], axis=0).T.astype(BF)


def run_copies(pairs, sems):
    copies = [pltpu.make_async_copy(a, b, sems.at[i]) for i, (a, b) in enumerate(pairs)]
    for cp in copies:
        cp.start()
    return copies


def wait_all(copies):
    for cp in copies:
        cp.wait()


def prep_queries(idx, q, ct, o0, o1, o2, o3, sems):
    pairs = []
    for d, out in enumerate((o0, o1, o2, o3)):
        rows = pl.ds(pl.multiple_of(lax.rem(idx[3] + d, NX) * GW, 16), GW)
        pairs += [(q.at[rows], out.at[0]), (ct.at[rows], out.at[1])]
    wait_all(run_copies(pairs, sems))


def live_mask(idx, shift):
    lane = lax.broadcasted_iota(jnp.int32, (1, TOK), 1)
    block = lax.rem(shift + lane // ROWS, NX)
    pos = idx[2] * TOK + block * ROWS + lane % ROWS
    return (pos < idx[4]).astype(F32)


def ones_row(v, row):
    pad = jnp.zeros((15, v.shape[1]), F32)
    return jnp.concatenate([v, row, pad], axis=0)


def project(
    idx, w0, w_prev, w_next, w_lo, w_hi, v0, v_prev, v_next, v_lo, v_hi,
    t0, t1, t3, t2_lo, t2_hi, kt, vt, summ, tbuf, acc,
):
    for i, off in enumerate((0, 3, 1, 2)):
        block = lax.rem(idx[2] + off, NY)
        start = pl.multiple_of(block * GW, 16)
        for d, t in ((0, t0), (1, t1), (3, t3)):
            tbuf[i, :, ROWS * d : ROWS * (d + 1)] = t[pl.ds(start, GW)]
        near = pl.multiple_of(lax.rem(block, 2) * GW, 16)
        for lo, t in ((True, t2_lo), (False, t2_hi)):

            @pl.when((block < 2) == lo)
            def _():
                tbuf[i, :, 2 * ROWS : 3 * ROWS] = t[pl.ds(near, GW)]

    c = idx[1]
    for g, ws in ((c, (w0, w_prev, w_next)), (1 - c, (v0, v_prev, v_next))):
        lo, hi = (w_lo, w_hi) if ws[0] is w0 else (v_lo, v_hi)
        far = jnp.concatenate([lo[...], hi[...]], axis=0)
        total = nn(far, tbuf[3])
        for i, w in enumerate(ws):
            total = total + nn(w[...], tbuf[i])
        acc[g] = total.astype(BF)
    live = live_mask(idx, idx[3])
    one = jnp.ones((1, TOK), F32)
    for h in range(GH):
        s = slice(HEAD_DIM * h, HEAD_DIM * (h + 1))
        keys = jnp.maximum(acc[0, s].astype(F32), 0.0)
        values = acc[1, s]
        kt[s] = keys.astype(BF)
        vt[s] = values
        vh = ones_row(values.astype(F32), one).astype(BF)
        summ[s] = nt((keys * live).astype(BF), vh).astype(BF)


def total_of(parts):
    total = parts[0][...].astype(F32)
    for p in parts[1:]:
        total = total + p[...].astype(F32)
    return total.astype(BF)


def query_side(idx, s0, s1, s2, s3, q0, q1, q2, q3, g0, g1, g2, g3, dsum):
    summ = total_of((s0, s1, s2, s3))
    live = live_mask(idx, idx[3])
    length = idx[4].astype(F32)
    for h in range(GH):
        s = slice(HEAD_DIM * h, HEAD_DIM * (h + 1))

        def pieces(k):
            at = slice(D // 2 + GW * k + s.start, D // 2 + GW * k + s.stop)
            parts = (q0[k, s], q1[at], q2[k, s], q3[at])
            return jnp.concatenate([p.astype(F32) for p in parts], axis=1)

        q = pieces(0)
        back = pieces(1) * live
        phi = jnp.maximum(q, 0.0)
        phib = phi.astype(BF)
        sh = summ[s]
        numer = tn(sh, phib)
        inv = 1.0 / (numer[HEAD_DIM : HEAD_DIM + 1] + length)
        dnum = back * inv
        dden = -jnp.sum(back * numer[:HEAD_DIM], axis=0, keepdims=True) * inv * inv
        ext = ones_row(dnum, dden).astype(BF)
        grad = jnp.where(q > 0, nn(sh, ext), 0.0).astype(BF)
        for d, g in enumerate((g0, g1, g2, g3)):
            g[s] = grad[:, ROWS * d : ROWS * (d + 1)]
        dsum[s] = nt(phib, ext).astype(BF)


def key_side(idx, s0, s1, s2, s3, kt, vt, dkt):
    summ = total_of((s0, s1, s2, s3))
    live = live_mask(idx, idx[3])
    one = jnp.ones((1, TOK), F32)
    for h in range(GH):
        s = slice(HEAD_DIM * h, HEAD_DIM * (h + 1))
        vh = ones_row(vt[s].astype(F32), one).astype(BF)
        dk = nn(summ[s], vh)
        keep = (kt[s].astype(F32) > 0) & (live > 0)
        dkt[s] = jnp.where(keep, dk, 0.0).astype(BF)


def group_tokens(idx, t0, t1, t3, t2_lo, t2_hi, own, oth, buf):
    for d, t in ((0, t0), (1, t1), (3, t3)):
        buf[:, ROWS * d : ROWS * (d + 1)] = t[...].astype(F32)
    buf[: D // 2, 2 * ROWS : 3 * ROWS] = t2_lo[: D // 2].astype(F32)
    buf[D // 2 :, 2 * ROWS : 3 * ROWS] = t2_hi[: D // 2].astype(F32)
    zero = jnp.zeros((PAD - HALF, TOK), F32)
    for c in range(2):

        @pl.when(idx[1] == c)
        def _():
            for i in range(16):
                base = SH * i
                for half, dst in ((c, own), (1 - c, oth)):
                    lo = base + HALF * half
                    rows = jnp.concatenate([buf[lo : lo + HALF], zero], axis=0)
                    dst[PAD * i : PAD * (i + 1)] = rows.astype(BF)


def grad_first(t, d, out):
    out[...] = nt(t[...], d[...])


def pack(p):
    extra = [p[PR:PAD, EX * j : EX * (j + 1)] for j in range(GW // EX)]
    extra.append(jnp.zeros((PAD - PR, EX), F32))
    return jnp.concatenate([p[:PR], jnp.concatenate(extra, axis=0)], axis=1)


def grad_second(idx, first, t, d, out):
    part = first[...] + nt(t[...], d[...])
    for y in range(NY):
        for x in range(NX):
            i = NX * y + x
            z = lax.rem(x - idx[3] + NX, NX)
            out[z * NY + y] = pack(part[PAD * i : PAD * (i + 1)]).astype(BF)


def sum_pieces(g, out):
    total = g[0].astype(F32)
    for i in range(1, 16):
        total = total + g[i].astype(F32)
    out[...] = total.astype(BF)


def place_rows(idx, r0, r1, r2, r3, o0, o1, o2, o3, out, buf):
    for step, (r, o) in enumerate(((r0, o0), (r1, o1), (r2, o2), (r3, o3))):
        k = lax.rem(idx[3] - idx[0] + step + NX, NX)
        buf[idx[1], k] = r[...].astype(F32)
        buf[1 - idx[1], k] = o[...].astype(F32)
    for c in range(2):
        for k in range(NX):
            lo, at = HALF * c, GW * k
            out[lo : lo + PR, at : at + GW] = buf[c, k, :, :GW]
            tail = [buf[c, k, 8 * j : 8 * (j + 1), GW:] for j in range(GW // EX)]
            tail = jnp.concatenate(tail, axis=1)
            out[lo + PR : lo + HALF, at : at + GW] = tail[: HALF - PR]


def place_queries(idx, g0, g1, g2, g3, out):
    for d, src in enumerate((g0, g1, g2, g3)):
        out[pl.ds(pl.multiple_of(lax.rem(idx[3] + d, NX) * GW, 16), GW)] = src[...]


def shift(v, axis, d, n=4):
    return lax.ppermute(v, axis, [(i, (i + d) % n) for i in range(n)])


def sds(shape, dtype=BF):
    return jax.ShapeDtypeStruct(shape, dtype)


def per_device(tokens, queries, cotangent, key_weight, value_weight, clip_len):
    z, c, y, x = (lax.axis_index(a) for a in ("z", "core", "y", "x"))
    idx = jnp.stack([z, c, y, x, clip_len[0]]).astype(jnp.int32)
    t_own, quers, backs = tokens[0].T, queries[0].T, cotangent[0].T

    def swap(v):
        return shift(v, "core", 1, 2)

    def sum_parts(s):
        return [s] + [shift(s, "y", d) for d in (1, 3, 2)]

    pieces = call(
        prep_weights,
        sds((NX, SH, GW)),
        [HBM, HBM],
        (key_weight, value_weight),
        scratch=[pltpu.VMEM((SH, D), BF), pltpu.SemaphoreType.DMA],
        vmem=60,
    )
    merged = lax.all_to_all(pieces, "x", 0, 0, tiled=True)
    t_own, _ = lax.optimization_barrier((t_own, pieces))
    qc = call(
        prep_queries,
        [sds((2, GW, ROWS))] * NX,
        [SMEM, ANY, ANY],
        (idx, quers, backs),
        scratch=[pltpu.SemaphoreType.DMA((8,))],
    )
    merged, *qc = lax.optimization_barrier((merged, *qc))
    t_late, _ = lax.optimization_barrier((t_own, merged))
    w_own = call(merge_weights, sds((GW, GW)), [VMEM], (merged,))
    w_prev = shift(w_own, "y", 1)
    w_next = shift(w_own, "y", -1)
    t_prev = shift(t_late, "x", 1)
    t_next = shift(t_own, "x", -1)
    f_lo = shift(w_prev[:SPLIT], "y", 1)
    f_hi = shift(w_next[SPLIT:], "y", -1)
    t_lo = shift(jnp.concatenate([t_prev[: D // 2], qc[1].reshape(2 * GW, ROWS)]), "x", 1)
    t_hi = shift(jnp.concatenate([t_next[D // 2 :], qc[3].reshape(2 * GW, ROWS)]), "x", -1)
    ts = (t_own, t_next, t_prev, t_lo, t_hi)
    g_own, g_oth = call(
        group_tokens,
        [sds((16 * PAD, TOK))] * 2,
        [SMEM] + [VMEM] * 5,
        (idx, *ts),
        scratch=[pltpu.VMEM((D, TOK), F32)],
        vmem=10,
        nbytes=10_000_000,
    )
    f_lo, f_hi, g_own, g_oth = lax.optimization_barrier((f_lo, f_hi, g_own, g_oth))
    ws = (w_own, w_prev, w_next, f_lo, f_hi)
    kt, vt, summ = call(
        project,
        [sds((GW, TOK)), sds((GW, TOK)), sds((GW, 128))],
        [SMEM] + [VMEM] * 15,
        (idx, *ws, *[swap(w) for w in ws], *ts),
        scratch=[pltpu.VMEM((NY, GW, TOK), BF), pltpu.VMEM((2, GW, TOK), BF)],
        vmem=16,
        flops=4 * TOK * D * GW,
        nbytes=5_000_000,
    )
    summ, far = lax.optimization_barrier((summ, qc[2]))
    parts = sum_parts(summ)
    q_in = (qc[0], t_hi, shift(far, "x", 2), t_lo)
    g_oth = swap(g_oth)

    outs = call(
        query_side,
        [sds((GW, ROWS))] * NX + [sds((GW, 128))],
        [SMEM] + [VMEM] * 8,
        (idx, *parts, *q_in),
        flops=6 * TOK * GW * 128,
        nbytes=4_000_000,
    )
    gq, dsum = outs[:NX], outs[NX]
    parts = sum_parts(dsum)
    g_in = [gq[0]]
    for d in (1, 2, 3):
        g_in.append(shift(gq[NX - d], "x", -d))
    dkt = call(
        key_side,
        sds((GW, TOK)),
        [SMEM] + [VMEM] * 6,
        (idx, *parts, kt, vt),
        flops=2 * TOK * GW * 128,
        nbytes=2_000_000,
    )
    first = call(
        grad_first,
        sds((16 * PAD, GW), F32),
        [VMEM] * 2,
        (g_own, dkt),
        flops=2 * 16 * PAD * TOK * GW,
        nbytes=5_000_000,
    )
    part = call(
        grad_second,
        sds((16, PR, PL)),
        [SMEM] + [VMEM] * 3,
        (idx, first, g_oth, swap(dkt)),
        flops=2 * 16 * PAD * TOK * GW,
        nbytes=5_000_000,
    )
    part = lax.all_to_all(part, ("z", "y"), 0, 0, tiled=True)
    grad_q = call(place_queries, sds((D, ROWS)), [SMEM] + [VMEM] * 4, (idx, *g_in))
    part, grad_q = lax.optimization_barrier((part, grad_q))
    rows = call(sum_pieces, sds((PR, PL)), [VMEM], (part,))
    got = [
        lax.ppermute(
            rows,
            ("z", "x"),
            [
                (z_at * NX + x_at, (z_at + s) % NZ * NX + (x_at + z_at) % NX)
                for z_at in range(NZ)
                for x_at in range(NX)
            ],
        )
        for s in range(NZ)
    ]
    grad_rows = call(
        place_rows,
        sds((SH, D), F32),
        [SMEM] + [VMEM] * 8,
        (idx, *got, *[swap(g) for g in got]),
        scratch=[pltpu.VMEM((2, NX, PR, PL), F32)],
    )
    return grad_q.T[None], grad_rows


def solution(mesh):
    grid = Mesh(mesh.devices.reshape(NZ, 2, NY, NX), ("z", "core", "y", "x"))
    dp, ctx = ("z", "core"), ("y", "x")
    in_specs = (
        P(dp, ctx, None),
        P(dp, ctx, None),
        P(dp, ctx, None),
        P(ctx, None),
        P(ctx, None),
        P(dp),
    )
    out_specs = (P(dp, ctx, None), P(ctx, None))
    return jax.shard_map(
        per_device, mesh=grid, in_specs=in_specs, out_specs=out_specs, check_vma=False
    )
```

```python
import jax
import jax.numpy as jnp
from jax import lax
from jax.experimental import pallas as pl
from jax.experimental.pallas import tpu as pltpu
from jax.sharding import Mesh
from jax.sharding import PartitionSpec as P

HEADS = 20
HEAD_DIM = 112
D = 2240
NX = 4
NY = 4
NZ = 4
GH = HEADS // NX
GW = GH * HEAD_DIM
ROWS = 128
TOK = ROWS * NX
SH = D // 16
HALF = SH // 2
PAD = 72
PR, PL = 64, 640
EX = PL - GW
SPLIT = 288
BF = jnp.bfloat16
F32 = jnp.float32
VMEM = pl.BlockSpec(memory_space=pltpu.VMEM)
SMEM = pl.BlockSpec(memory_space=pltpu.SMEM)
ANY = pl.BlockSpec(memory_space=pl.ANY)
HBM = pl.BlockSpec(memory_space=pltpu.HBM)


def params(vmem):
    return pltpu.CompilerParams(vmem_limit_bytes=vmem * 1024 * 1024)


def call(body, out_shape, in_specs, args, scratch=(), flops=0, nbytes=0, name=None, vmem=6):
    return pl.pallas_call(
        body,
        out_shape=out_shape,
        in_specs=in_specs,
        out_specs=jax.tree.map(lambda _: VMEM, out_shape),
        scratch_shapes=list(scratch),
        compiler_params=params(vmem),
        cost_estimate=pl.CostEstimate(flops=flops, bytes_accessed=nbytes, transcendentals=0),
        name=name,
    )(*args)


def nt(a, b):
    return lax.dot_general(a, b, (((1,), (1,)), ((), ())), preferred_element_type=F32)


def tn(a, b):
    return lax.dot_general(a, b, (((0,), (0,)), ((), ())), preferred_element_type=F32)


def nn(a, b):
    return jnp.dot(a, b, preferred_element_type=F32)


def prep_weights(wk, wv, out, buf, sem):
    core = lax.axis_index("core")
    for c, src in ((0, wk), (1, wv)):

        @pl.when(core == c)
        def _():
            cp = pltpu.make_async_copy(src, buf, sem)
            cp.start()
            cp.wait()

    for k in range(NX):
        out[k] = buf[:, GW * k : GW * (k + 1)]


def merge_weights(g, full):
    w = jnp.concatenate([g[k].astype(F32) for k in range(NX)], axis=0).T
    full[:, :GW] = w.astype(BF)
    full[:, GW:] = jnp.zeros((GW, PL - GW), BF)


def run_copies(pairs, sems):
    copies = [pltpu.make_async_copy(a, b, sems.at[i]) for i, (a, b) in enumerate(pairs)]
    for cp in copies:
        cp.start()
    return copies


def wait_all(copies):
    for cp in copies:
        cp.wait()


def prep_queries(idx, q, ct, o0, o1, o2, o3, sems):
    pairs = []
    for d, out in enumerate((o0, o1, o2, o3)):
        rows = pl.ds(pl.multiple_of(lax.rem(idx[3] + d, NX) * GW, 16), GW)
        pairs += [(q.at[rows], out.at[0]), (ct.at[rows], out.at[1])]
    wait_all(run_copies(pairs, sems))


def live_mask(idx, shift):
    lane = lax.broadcasted_iota(jnp.int32, (1, TOK), 1)
    block = lax.rem(shift + lane // ROWS, NX)
    pos = idx[2] * TOK + block * ROWS + lane % ROWS
    return (pos < idx[4]).astype(F32)


def ones_row(v, row):
    pad = jnp.zeros((15, v.shape[1]), F32)
    return jnp.concatenate([v, row, pad], axis=0)


def project(
    idx, w0, w_prev, w_next, w_lo, w_hi, v0, v_prev, v_next, v_lo, v_hi,
    t0, t1, t3, t2_lo, t2_hi, kt, vt, summ, tbuf, acc,
):
    for i, off in enumerate((0, 3, 1, 2)):
        block = lax.rem(idx[2] + off, NY)
        start = pl.multiple_of(block * GW, 16)
        at = PL * i
        for d, t in ((0, t0), (1, t1), (3, t3)):
            tbuf[at : at + GW, ROWS * d : ROWS * (d + 1)] = t[pl.ds(start, GW)]
        near = pl.multiple_of(lax.rem(block, 2) * GW, 16)
        for lo, t in ((True, t2_lo), (False, t2_hi)):

            @pl.when((block < 2) == lo)
            def _():
                tbuf[at : at + GW, 2 * ROWS : 3 * ROWS] = t[pl.ds(near, GW)]

        tbuf[at + GW : at + PL] = jnp.zeros((PL - GW, TOK), BF)

    c = idx[1]
    for g, ws, halves in (
        (c, (w0, w_prev, w_next), (w_lo, w_hi)),
        (1 - c, (v0, v_prev, v_next), (v_lo, v_hi)),
    ):
        far = jnp.concatenate([r[...] for r in halves], axis=0)
        rows = jnp.concatenate([w[...] for w in ws] + [far], axis=1)
        acc[g] = nn(rows, tbuf[...]).astype(BF)
    live = live_mask(idx, idx[3])
    one = jnp.ones((1, TOK), F32)
    for h in range(GH):
        s = slice(HEAD_DIM * h, HEAD_DIM * (h + 1))
        keys = jnp.maximum(acc[0, s].astype(F32), 0.0)
        values = acc[1, s]
        kt[s] = keys.astype(BF)
        vt[s] = values
        vh = ones_row(values.astype(F32), one).astype(BF)
        summ[s] = nt((keys * live).astype(BF), vh).astype(BF)


def total_of(parts):
    total = parts[0][...].astype(F32)
    for p in parts[1:]:
        total = total + p[...].astype(F32)
    return total.astype(BF)


def query_side(idx, s0, s1, s2, s3, q0, q1, q2, q3, g0, g1, g2, g3, dsum):
    summ = total_of((s0, s1, s2, s3))
    live = live_mask(idx, idx[3])
    length = idx[4].astype(F32)
    for h in range(GH):
        s = slice(HEAD_DIM * h, HEAD_DIM * (h + 1))

        def pieces(k):
            at = slice(D // 2 + GW * k + s.start, D // 2 + GW * k + s.stop)
            parts = (q0[k, s], q1[at], q2[k, s], q3[at])
            return jnp.concatenate([p.astype(F32) for p in parts], axis=1)

        q = pieces(0)
        back = pieces(1) * live
        phi = jnp.maximum(q, 0.0)
        phib = phi.astype(BF)
        sh = summ[s]
        numer = tn(sh, phib)
        inv = 1.0 / (numer[HEAD_DIM : HEAD_DIM + 1] + length)
        dnum = back * inv
        dden = -jnp.sum(back * numer[:HEAD_DIM], axis=0, keepdims=True) * inv * inv
        ext = ones_row(dnum, dden).astype(BF)
        grad = jnp.where(q > 0, nn(sh, ext), 0.0).astype(BF)
        for d, g in enumerate((g0, g1, g2, g3)):
            g[s] = grad[:, ROWS * d : ROWS * (d + 1)]
        dsum[s] = nt(phib, ext).astype(BF)


def key_side(idx, s0, s1, s2, s3, kt, vt, dkt):
    summ = total_of((s0, s1, s2, s3))
    live = live_mask(idx, idx[3])
    one = jnp.ones((1, TOK), F32)
    for h in range(GH):
        s = slice(HEAD_DIM * h, HEAD_DIM * (h + 1))
        vh = ones_row(vt[s].astype(F32), one).astype(BF)
        dk = nn(summ[s], vh)
        keep = (kt[s].astype(F32) > 0) & (live > 0)
        dkt[s] = jnp.where(keep, dk, 0.0).astype(BF)


def group_tokens(idx, t0, t1, t3, t2_lo, t2_hi, own, oth, buf):
    for d, t in ((0, t0), (1, t1), (3, t3)):
        buf[:, ROWS * d : ROWS * (d + 1)] = t[...].astype(F32)
    buf[: D // 2, 2 * ROWS : 3 * ROWS] = t2_lo[: D // 2].astype(F32)
    buf[D // 2 :, 2 * ROWS : 3 * ROWS] = t2_hi[: D // 2].astype(F32)
    zero = jnp.zeros((PAD - HALF, TOK), F32)
    for c in range(2):

        @pl.when(idx[1] == c)
        def _():
            for i in range(16):
                base = SH * i
                for half, dst in ((c, own), (1 - c, oth)):
                    lo = base + HALF * half
                    rows = jnp.concatenate([buf[lo : lo + HALF], zero], axis=0)
                    dst[PAD * i : PAD * (i + 1)] = rows.astype(BF)


def grad_first(t, d, out):
    out[...] = nt(t[...], d[...])


def pack(p):
    extra = [p[PR:PAD, EX * j : EX * (j + 1)] for j in range(GW // EX)]
    extra.append(jnp.zeros((PAD - PR, EX), F32))
    return jnp.concatenate([p[:PR], jnp.concatenate(extra, axis=0)], axis=1)


def grad_second(idx, first, t, d, out):
    part = first[...] + nt(t[...], d[...])
    for y in range(NY):
        for x in range(NX):
            i = NX * y + x
            z = lax.rem(x - idx[3] + NX, NX)
            out[z * NY + y] = pack(part[PAD * i : PAD * (i + 1)]).astype(BF)


def sum_pieces(g, out):
    total = g[0].astype(F32)
    for i in range(1, 16):
        total = total + g[i].astype(F32)
    out[...] = total.astype(BF)


def place_rows(idx, r0, r1, r2, r3, o0, o1, o2, o3, out, buf):
    for step, (r, o) in enumerate(((r0, o0), (r1, o1), (r2, o2), (r3, o3))):
        k = lax.rem(idx[3] - idx[0] + step + NX, NX)
        buf[idx[1], k] = r[...].astype(F32)
        buf[1 - idx[1], k] = o[...].astype(F32)
    for c in range(2):
        for k in range(NX):
            lo, at = HALF * c, GW * k
            out[lo : lo + PR, at : at + GW] = buf[c, k, :, :GW]
            tail = [buf[c, k, 8 * j : 8 * (j + 1), GW:] for j in range(GW // EX)]
            tail = jnp.concatenate(tail, axis=1)
            out[lo + PR : lo + HALF, at : at + GW] = tail[: HALF - PR]


def place_queries(idx, g0, g1, g2, g3, out):
    for d, src in enumerate((g0, g1, g2, g3)):
        out[pl.ds(pl.multiple_of(lax.rem(idx[3] + d, NX) * GW, 16), GW)] = src[...]


def shift(v, axis, d, n=4):
    return lax.ppermute(v, axis, [(i, (i + d) % n) for i in range(n)])


def sds(shape, dtype=BF):
    return jax.ShapeDtypeStruct(shape, dtype)


def per_device(tokens, queries, cotangent, key_weight, value_weight, clip_len):
    z, c, y, x = (lax.axis_index(a) for a in ("z", "core", "y", "x"))
    idx = jnp.stack([z, c, y, x, clip_len[0]]).astype(jnp.int32)
    t_own, quers, backs = tokens[0].T, queries[0].T, cotangent[0].T

    def swap(v):
        return shift(v, "core", 1, 2)

    def sum_parts(s):
        return [s] + [shift(s, "y", d) for d in (1, 3, 2)]

    pieces = call(
        prep_weights,
        sds((NX, SH, GW)),
        [HBM, HBM],
        (key_weight, value_weight),
        scratch=[pltpu.VMEM((SH, D), BF), pltpu.SemaphoreType.DMA],
        vmem=60,
    )
    merged = lax.all_to_all(pieces, "x", 0, 0, tiled=True)
    t_own, _ = lax.optimization_barrier((t_own, pieces))
    qc = call(
        prep_queries,
        [sds((2, GW, ROWS))] * NX,
        [SMEM, ANY, ANY],
        (idx, quers, backs),
        scratch=[pltpu.SemaphoreType.DMA((8,))],
    )
    merged, *qc = lax.optimization_barrier((merged, *qc))
    t_late, _ = lax.optimization_barrier((t_own, merged))
    w_own = call(merge_weights, sds((GW, PL)), [VMEM], (merged,))
    w_prev = shift(w_own, "y", 1)
    w_next = shift(w_own, "y", -1)
    t_prev = shift(t_late, "x", 1)
    t_next = shift(t_own, "x", -1)
    f_lo = shift(w_prev[:SPLIT], "y", 1)
    f_hi = shift(w_next[SPLIT:], "y", -1)
    t_lo = shift(jnp.concatenate([t_prev[: D // 2], qc[1].reshape(2 * GW, ROWS)]), "x", 1)
    t_hi = shift(jnp.concatenate([t_next[D // 2 :], qc[3].reshape(2 * GW, ROWS)]), "x", -1)
    ts = (t_own, t_next, t_prev, t_lo, t_hi)
    g_own, g_oth = call(
        group_tokens,
        [sds((16 * PAD, TOK))] * 2,
        [SMEM] + [VMEM] * 5,
        (idx, *ts),
        scratch=[pltpu.VMEM((D, TOK), F32)],
        vmem=10,
        nbytes=10_000_000,
    )
    f_lo, f_hi, g_own, g_oth = lax.optimization_barrier((f_lo, f_hi, g_own, g_oth))
    ws = (w_own, w_prev, w_next, f_lo, f_hi)
    kt, vt, summ = call(
        project,
        [sds((GW, TOK)), sds((GW, TOK)), sds((GW, 128))],
        [SMEM] + [VMEM] * 15,
        (idx, *ws, *[swap(w) for w in ws], *ts),
        scratch=[pltpu.VMEM((NY * PL, TOK), BF), pltpu.VMEM((2, GW, TOK), BF)],
        vmem=16,
        flops=4 * TOK * D * GW,
        nbytes=5_000_000,
    )
    far, _, _ = lax.optimization_barrier((qc[2], t_lo, t_hi))
    parts = sum_parts(summ)
    q_in = (qc[0], t_hi, shift(far, "x", 2), t_lo)
    g_oth = swap(g_oth)

    outs = call(
        query_side,
        [sds((GW, ROWS))] * NX + [sds((GW, 128))],
        [SMEM] + [VMEM] * 8,
        (idx, *parts, *q_in),
        flops=6 * TOK * GW * 128,
        nbytes=4_000_000,
    )
    gq, dsum = outs[:NX], outs[NX]
    parts = sum_parts(dsum)
    g_in = [gq[0]]
    for d in (1, 2, 3):
        g_in.append(shift(gq[NX - d], "x", -d))
    dkt = call(
        key_side,
        sds((GW, TOK)),
        [SMEM] + [VMEM] * 6,
        (idx, *parts, kt, vt),
        flops=2 * TOK * GW * 128,
        nbytes=2_000_000,
    )
    first = call(
        grad_first,
        sds((16 * PAD, GW), F32),
        [VMEM] * 2,
        (g_own, dkt),
        flops=2 * 16 * PAD * TOK * GW,
        nbytes=5_000_000,
    )
    part = call(
        grad_second,
        sds((16, PR, PL)),
        [SMEM] + [VMEM] * 3,
        (idx, first, g_oth, swap(dkt)),
        flops=2 * 16 * PAD * TOK * GW,
        nbytes=5_000_000,
    )
    part = lax.all_to_all(part, ("z", "y"), 0, 0, tiled=True)
    grad_q = call(place_queries, sds((D, ROWS)), [SMEM] + [VMEM] * 4, (idx, *g_in))
    part, grad_q = lax.optimization_barrier((part, grad_q))
    rows = call(sum_pieces, sds((PR, PL)), [VMEM], (part,))
    got = [
        lax.ppermute(
            rows,
            ("z", "x"),
            [
                (z_at * NX + x_at, (z_at + s) % NZ * NX + (x_at + z_at) % NX)
                for z_at in range(NZ)
                for x_at in range(NX)
            ],
        )
        for s in range(NZ)
    ]
    grad_rows = call(
        place_rows,
        sds((SH, D), F32),
        [SMEM] + [VMEM] * 8,
        (idx, *got, *[swap(g) for g in got]),
        scratch=[pltpu.VMEM((2, NX, PR, PL), F32)],
    )
    return grad_q.T[None], grad_rows


def solution(mesh):
    grid = Mesh(mesh.devices.reshape(NZ, 2, NY, NX), ("z", "core", "y", "x"))
    dp, ctx = ("z", "core"), ("y", "x")
    in_specs = (
        P(dp, ctx, None),
        P(dp, ctx, None),
        P(dp, ctx, None),
        P(ctx, None),
        P(ctx, None),
        P(dp),
    )
    out_specs = (P(dp, ctx, None), P(ctx, None))
    return jax.shard_map(
        per_device, mesh=grid, in_specs=in_specs, out_specs=out_specs, check_vma=False
    )
```

```python
import jax
import jax.numpy as jnp
from jax import lax
from jax.experimental import pallas as pl
from jax.experimental.pallas import tpu as pltpu
from jax.sharding import Mesh
from jax.sharding import PartitionSpec as P

HEADS = 20
HEAD_DIM = 112
D = 2240
NX = 4
NY = 4
NZ = 4
GH = HEADS // NX
GW = GH * HEAD_DIM
ROWS = 128
TOK = ROWS * NX
SH = D // 16
HALF = SH // 2
PAD = 72
PR, PL = 64, 640
EX = PL - GW
SPLIT = 288
BF = jnp.bfloat16
F32 = jnp.float32
VMEM = pl.BlockSpec(memory_space=pltpu.VMEM)
SMEM = pl.BlockSpec(memory_space=pltpu.SMEM)
ANY = pl.BlockSpec(memory_space=pl.ANY)
HBM = pl.BlockSpec(memory_space=pltpu.HBM)


def params(vmem):
    return pltpu.CompilerParams(vmem_limit_bytes=vmem * 1024 * 1024)


def call(body, out_shape, in_specs, args, scratch=(), flops=0, nbytes=0, name=None, vmem=6):
    return pl.pallas_call(
        body,
        out_shape=out_shape,
        in_specs=in_specs,
        out_specs=jax.tree.map(lambda _: VMEM, out_shape),
        scratch_shapes=list(scratch),
        compiler_params=params(vmem),
        cost_estimate=pl.CostEstimate(flops=flops, bytes_accessed=nbytes, transcendentals=0),
        name=name,
    )(*args)


def nt(a, b):
    return lax.dot_general(a, b, (((1,), (1,)), ((), ())), preferred_element_type=F32)


def tn(a, b):
    return lax.dot_general(a, b, (((0,), (0,)), ((), ())), preferred_element_type=F32)


def nn(a, b):
    return jnp.dot(a, b, preferred_element_type=F32)


def prep_weights(wk, wv, out, buf, sem):
    core = lax.axis_index("core")
    for c, src in ((0, wk), (1, wv)):

        @pl.when(core == c)
        def _():
            cp = pltpu.make_async_copy(src, buf, sem)
            cp.start()
            cp.wait()

    for k in range(NX):
        out[k] = buf[:, GW * k : GW * (k + 1)]


def merge_weights(g, full):
    w = jnp.concatenate([g[k].astype(F32) for k in range(NX)], axis=0).T
    full[:, :GW] = w.astype(BF)
    full[:, GW:] = jnp.zeros((GW, PL - GW), BF)


def run_copies(pairs, sems):
    copies = [pltpu.make_async_copy(a, b, sems.at[i]) for i, (a, b) in enumerate(pairs)]
    for cp in copies:
        cp.start()
    return copies


def wait_all(copies):
    for cp in copies:
        cp.wait()


def prep_queries(idx, q, ct, o0, o1, o2, o3, sems):
    pairs = []
    for d, out in enumerate((o0, o1, o2, o3)):
        rows = pl.ds(pl.multiple_of(lax.rem(idx[3] + d, NX) * GW, 16), GW)
        pairs += [(q.at[rows], out.at[0]), (ct.at[rows], out.at[1])]
    wait_all(run_copies(pairs, sems))


def live_mask(idx, shift):
    lane = lax.broadcasted_iota(jnp.int32, (1, TOK), 1)
    block = lax.rem(shift + lane // ROWS, NX)
    pos = idx[2] * TOK + block * ROWS + lane % ROWS
    return (pos < idx[4]).astype(F32)


def ones_row(v, row):
    pad = jnp.zeros((15, v.shape[1]), F32)
    return jnp.concatenate([v, row, pad], axis=0)


def project(
    idx, w0, w_prev, w_next, w_lo, w_hi, v0, v_prev, v_next, v_lo, v_hi,
    t0, t1, t3, t2_lo, t2_hi, kt, vt, summ, tbuf, acc,
):
    for i, off in enumerate((0, 3, 1, 2)):
        block = lax.rem(idx[2] + off, NY)
        start = pl.multiple_of(block * GW, 16)
        at = PL * i
        for d, t in ((0, t0), (1, t1), (3, t3)):
            tbuf[at : at + GW, ROWS * d : ROWS * (d + 1)] = t[pl.ds(start, GW)]
        near = pl.multiple_of(lax.rem(block, 2) * GW, 16)
        for lo, t in ((True, t2_lo), (False, t2_hi)):

            @pl.when((block < 2) == lo)
            def _():
                tbuf[at : at + GW, 2 * ROWS : 3 * ROWS] = t[pl.ds(near, GW)]

        tbuf[at + GW : at + PL] = jnp.zeros((PL - GW, TOK), BF)

    c = idx[1]
    for g, ws, halves in (
        (c, (w0, w_prev, w_next), (w_lo, w_hi)),
        (1 - c, (v0, v_prev, v_next), (v_lo, v_hi)),
    ):
        far = jnp.concatenate([r[...] for r in halves], axis=0)
        rows = jnp.concatenate([w[...] for w in ws] + [far], axis=1)
        acc[g] = nn(rows, tbuf[...]).astype(BF)
    live = live_mask(idx, idx[3])
    one = jnp.ones((1, TOK), F32)
    for h in range(GH):
        s = slice(HEAD_DIM * h, HEAD_DIM * (h + 1))
        keys = jnp.maximum(acc[0, s].astype(F32), 0.0)
        values = acc[1, s]
        kt[s] = keys.astype(BF)
        vt[s] = values
        vh = ones_row(values.astype(F32), one).astype(BF)
        summ[s] = nt((keys * live).astype(BF), vh).astype(BF)


def total_of(parts):
    total = parts[0][...].astype(F32)
    for p in parts[1:]:
        total = total + p[...].astype(F32)
    return total.astype(BF)


def query_side(idx, s0, s1, s2, s3, q0, q1, q2, q3, g0, g1, g2, g3, dsum):
    summ = total_of((s0, s1, s2, s3))
    live = live_mask(idx, idx[3])
    length = idx[4].astype(F32)
    for h in range(GH):
        s = slice(HEAD_DIM * h, HEAD_DIM * (h + 1))

        def pieces(k):
            at = slice(D // 2 + GW * k + s.start, D // 2 + GW * k + s.stop)
            parts = (q0[k, s], q1[at], q2[k, s], q3[at])
            return jnp.concatenate([p.astype(F32) for p in parts], axis=1)

        q = pieces(0)
        back = pieces(1) * live
        phi = jnp.maximum(q, 0.0)
        phib = phi.astype(BF)
        sh = summ[s]
        numer = tn(sh, phib)
        inv = 1.0 / (numer[HEAD_DIM : HEAD_DIM + 1] + length)
        dnum = back * inv
        dden = -jnp.sum(back * numer[:HEAD_DIM], axis=0, keepdims=True) * inv * inv
        ext = ones_row(dnum, dden).astype(BF)
        grad = jnp.where(q > 0, nn(sh, ext), 0.0).astype(BF)
        for d, g in enumerate((g0, g1, g2, g3)):
            g[s] = grad[:, ROWS * d : ROWS * (d + 1)]
        dsum[s] = nt(phib, ext).astype(BF)


def key_side(idx, s0, s1, s2, s3, kt, vt, dkt):
    summ = total_of((s0, s1, s2, s3))
    live = live_mask(idx, idx[3])
    one = jnp.ones((1, TOK), F32)
    for h in range(GH):
        s = slice(HEAD_DIM * h, HEAD_DIM * (h + 1))
        vh = ones_row(vt[s].astype(F32), one).astype(BF)
        dk = nn(summ[s], vh)
        keep = (kt[s].astype(F32) > 0) & (live > 0)
        dkt[s] = jnp.where(keep, dk, 0.0).astype(BF)


def group_tokens(idx, t0, t1, t3, t2_lo, t2_hi, own, oth, buf):
    for d, t in ((0, t0), (1, t1), (3, t3)):
        buf[:, ROWS * d : ROWS * (d + 1)] = t[...].astype(F32)
    buf[: D // 2, 2 * ROWS : 3 * ROWS] = t2_lo[: D // 2].astype(F32)
    buf[D // 2 :, 2 * ROWS : 3 * ROWS] = t2_hi[: D // 2].astype(F32)
    zero = jnp.zeros((PAD - HALF, TOK), F32)
    for c in range(2):

        @pl.when(idx[1] == c)
        def _():
            for i in range(16):
                base = SH * i
                for half, dst in ((c, own), (1 - c, oth)):
                    lo = base + HALF * half
                    rows = jnp.concatenate([buf[lo : lo + HALF], zero], axis=0)
                    dst[PAD * i : PAD * (i + 1)] = rows.astype(BF)


def grad_first(t, d, out):
    out[...] = nt(t[...], d[...])


def pack(p):
    extra = [p[PR:PAD, EX * j : EX * (j + 1)] for j in range(GW // EX)]
    extra.append(jnp.zeros((PAD - PR, EX), F32))
    return jnp.concatenate([p[:PR], jnp.concatenate(extra, axis=0)], axis=1)


def grad_second(idx, first, t, d, out):
    part = first[...] + nt(t[...], d[...])
    for y in range(NY):
        for x in range(NX):
            i = NX * y + x
            z = lax.rem(x - idx[3] + NX, NX)
            out[z * NY + y] = pack(part[PAD * i : PAD * (i + 1)]).astype(BF)


def sum_pieces(g, out):
    total = g[0].astype(F32)
    for i in range(1, 16):
        total = total + g[i].astype(F32)
    out[...] = total.astype(BF)


def place_rows(idx, r0, r1, r2, r3, o0, o1, o2, o3, out, buf):
    for step, (r, o) in enumerate(((r0, o0), (r1, o1), (r2, o2), (r3, o3))):
        k = lax.rem(idx[3] - idx[0] + step + NX, NX)
        buf[idx[1], k] = r[...]
        buf[1 - idx[1], k] = o[...]
    for c in range(2):
        for k in range(NX):
            lo, at = HALF * c, GW * k
            block = buf[c, k].astype(F32)
            out[lo : lo + PR, at : at + GW] = block[:, :GW]
            tail = [block[8 * j : 8 * (j + 1), GW:] for j in range(GW // EX)]
            tail = jnp.concatenate(tail, axis=1)
            out[lo + PR : lo + HALF, at : at + GW] = tail[: HALF - PR]


def place_queries(idx, g0, g1, g2, g3, out):
    for d, src in enumerate((g0, g1, g2, g3)):
        out[pl.ds(pl.multiple_of(lax.rem(idx[3] + d, NX) * GW, 16), GW)] = src[...]


def shift(v, axis, d, n=4):
    return lax.ppermute(v, axis, [(i, (i + d) % n) for i in range(n)])


def sds(shape, dtype=BF):
    return jax.ShapeDtypeStruct(shape, dtype)


def per_device(tokens, queries, cotangent, key_weight, value_weight, clip_len):
    z, c, y, x = (lax.axis_index(a) for a in ("z", "core", "y", "x"))
    idx = jnp.stack([z, c, y, x, clip_len[0]]).astype(jnp.int32)
    t_own, quers, backs = tokens[0].T, queries[0].T, cotangent[0].T

    def swap(v):
        return shift(v, "core", 1, 2)

    def sum_parts(s):
        return [s] + [shift(s, "y", d) for d in (1, 3, 2)]

    pieces = call(
        prep_weights,
        sds((NX, SH, GW)),
        [HBM, HBM],
        (key_weight, value_weight),
        scratch=[pltpu.VMEM((SH, D), BF), pltpu.SemaphoreType.DMA],
        vmem=60,
    )
    merged = lax.all_to_all(pieces, "x", 0, 0, tiled=True)
    t_own, _ = lax.optimization_barrier((t_own, pieces))
    qc = call(
        prep_queries,
        [sds((2, GW, ROWS))] * NX,
        [SMEM, ANY, ANY],
        (idx, quers, backs),
        scratch=[pltpu.SemaphoreType.DMA((8,))],
    )
    merged, *qc = lax.optimization_barrier((merged, *qc))
    t_late, _ = lax.optimization_barrier((t_own, merged))
    w_own = call(merge_weights, sds((GW, PL)), [VMEM], (merged,))
    w_prev = shift(w_own, "y", 1)
    w_next = shift(w_own, "y", -1)
    t_prev = shift(t_late, "x", 1)
    t_next = shift(t_own, "x", -1)
    f_lo = shift(w_prev[:SPLIT], "y", 1)
    f_hi = shift(w_next[SPLIT:], "y", -1)
    t_lo = shift(jnp.concatenate([t_prev[: D // 2], qc[1].reshape(2 * GW, ROWS)]), "x", 1)
    t_hi = shift(jnp.concatenate([t_next[D // 2 :], qc[3].reshape(2 * GW, ROWS)]), "x", -1)
    ts = (t_own, t_next, t_prev, t_lo, t_hi)
    g_own, g_oth = call(
        group_tokens,
        [sds((16 * PAD, TOK))] * 2,
        [SMEM] + [VMEM] * 5,
        (idx, *ts),
        scratch=[pltpu.VMEM((D, TOK), F32)],
        vmem=10,
        nbytes=10_000_000,
    )
    f_lo, f_hi, g_own, g_oth = lax.optimization_barrier((f_lo, f_hi, g_own, g_oth))
    ws = (w_own, w_prev, w_next, f_lo, f_hi)
    kt, vt, summ = call(
        project,
        [sds((GW, TOK)), sds((GW, TOK)), sds((GW, 128))],
        [SMEM] + [VMEM] * 15,
        (idx, *ws, *[swap(w) for w in ws], *ts),
        scratch=[pltpu.VMEM((NY * PL, TOK), BF), pltpu.VMEM((2, GW, TOK), BF)],
        vmem=16,
        flops=4 * TOK * D * GW,
        nbytes=5_000_000,
    )
    far, _, _ = lax.optimization_barrier((qc[2], t_lo, t_hi))
    parts = sum_parts(summ)
    q_in = (qc[0], t_hi, shift(far, "x", 2), t_lo)
    g_oth = swap(g_oth)

    outs = call(
        query_side,
        [sds((GW, ROWS))] * NX + [sds((GW, 128))],
        [SMEM] + [VMEM] * 8,
        (idx, *parts, *q_in),
        flops=6 * TOK * GW * 128,
        nbytes=4_000_000,
    )
    gq, dsum = outs[:NX], outs[NX]
    parts = sum_parts(dsum)
    g_in = [gq[0]]
    for d in (1, 2, 3):
        g_in.append(shift(gq[NX - d], "x", -d))
    dkt = call(
        key_side,
        sds((GW, TOK)),
        [SMEM] + [VMEM] * 6,
        (idx, *parts, kt, vt),
        flops=2 * TOK * GW * 128,
        nbytes=2_000_000,
    )
    first = call(
        grad_first,
        sds((16 * PAD, GW), F32),
        [VMEM] * 2,
        (g_own, dkt),
        flops=2 * 16 * PAD * TOK * GW,
        nbytes=5_000_000,
    )
    part = call(
        grad_second,
        sds((16, PR, PL)),
        [SMEM] + [VMEM] * 3,
        (idx, first, g_oth, swap(dkt)),
        flops=2 * 16 * PAD * TOK * GW,
        nbytes=5_000_000,
    )
    part = lax.all_to_all(part, ("z", "y"), 0, 0, tiled=True)
    grad_q = call(place_queries, sds((D, ROWS)), [SMEM] + [VMEM] * 4, (idx, *g_in))
    part, grad_q = lax.optimization_barrier((part, grad_q))
    rows = call(sum_pieces, sds((PR, PL)), [VMEM], (part,))
    got = {}
    for s in (0, 1, 3, 2):
        pairs = [
            (z_at * NX + x_at, (z_at + s) % NZ * NX + (x_at + z_at) % NX)
            for z_at in range(NZ)
            for x_at in range(NX)
        ]
        got[s] = lax.ppermute(rows, ("z", "x"), pairs)
    got = [got[s] for s in range(NZ)]
    grad_rows = call(
        place_rows,
        sds((SH, D), F32),
        [SMEM] + [VMEM] * 8,
        (idx, *got, *[swap(g) for g in got]),
        scratch=[pltpu.VMEM((2, NX, PR, PL), BF)],
    )
    return grad_q.T[None], grad_rows


def solution(mesh):
    grid = Mesh(mesh.devices.reshape(NZ, 2, NY, NX), ("z", "core", "y", "x"))
    dp, ctx = ("z", "core"), ("y", "x")
    in_specs = (
        P(dp, ctx, None),
        P(dp, ctx, None),
        P(dp, ctx, None),
        P(ctx, None),
        P(ctx, None),
        P(dp),
    )
    out_specs = (P(dp, ctx, None), P(ctx, None))
    return jax.shard_map(
        per_device, mesh=grid, in_specs=in_specs, out_specs=out_specs, check_vma=False
    )
```
